32 devices in a mesh: row: 16 (over z, y, x), rep: 2 (over core).
Axes of the slice: x: 2, y: 2, z: 4, core: 2. Of those that a mesh axis runs over, the one named last changes fastest.
Arguments:
- features: bfloat16 [8192, 256], P('row'), may hold values from -6 to 6
- weight: bfloat16 [256, 256], replicated, may hold values from -0.375 to 0.375
- bias: float32 [256], replicated, may hold values from -3 to 3
- cotangent: bfloat16 [8192, 256], P(('row', 'rep')), may hold values from -14 to 14
- tile_values: bfloat16 [16, 16, 8, 128, 128], P('row', 'rep'), may hold values from -0.125 to 0.125
- tile_index: int32 [16, 16, 8, 2], P('row', 'rep'), may hold values from 0 to 3
- tile_count: int32 [16, 16], P('row', 'rep'), may hold values from 0 to 8, as said below
- rev_values: bfloat16 [16, 16, 8, 128, 128], P('row', 'rep'), may hold values from -0.125 to 0.125
- rev_index: int32 [16, 16, 8, 2], P('row', 'rep'), may hold values from 0 to 3
- rev_count: int32 [16, 16], P('row', 'rep'), may hold values from 0 to 8, as said below
Outputs:
- activations: bfloat16 [8192, 256], P(('row', 'rep'))
- grad_features: bfloat16 [8192, 256], P(('row', 'rep'))
- grad_weight: float32 [256, 256], replicated
- grad_bias: float32 [256], replicated
The draws below stay inside these ranges and needn't reach their ends.
Inputs may be any that keep to these rules, and one draw needn't show every extreme that they name: Slots t < tile_count[a, d] are used; some slab pair uses all 8 slots in every draw. Slots t < rev_count[a, d] are used; some slab pair uses all 8 slots in every draw.
All inputs are finite; a program needn't handle non-finite values.
Results may differ from the reference program's by a relative error of at most 0.006.
Values may be sent and summed in bfloat16 or wider, within the bound.
A program may use at most 64 MiB of HBM per device.

```python
import jax
import jax.numpy as jnp
from jax import lax

WIDTH = 256
TILE = 128
BLOCKS = 4
SLOTS = 8
SLABS = 16
NODES = 8192


def skewed_counts(key):
    first, second, third = jax.random.split(key, 3)
    heavy_slab = jax.random.randint(first, (SLABS,), 0, 4) == 0
    forced = jax.random.randint(second, (), 0, SLABS)
    heavy_slab = heavy_slab | (jnp.arange(SLABS) == forced)
    base = jax.random.randint(third, (SLABS, SLABS), 0, SLOTS // 2 + 1)
    partner = (jnp.arange(SLABS)[:, None] + jnp.arange(SLABS)[None, :]) % SLABS
    heavy_pair = heavy_slab[:, None] | heavy_slab[partner]
    return jnp.where(heavy_pair, SLOTS, base).astype(jnp.int32)


def draw_tile_count(key, part):
    return skewed_counts(jax.random.fold_in(key, 11))


def draw_rev_count(key, part):
    return skewed_counts(jax.random.fold_in(key, 23))


def draw_cotangent(key, part):
    first = jax.random.fold_in(jax.random.fold_in(key, 37), 0)
    rows = jnp.arange(NODES, dtype=jnp.float32)[:, None] / float(NODES)
    noise = jnp.clip(jax.random.normal(first, (NODES, WIDTH), jnp.float32), -4.0, 4.0)
    values = noise * jnp.power(3.0, rows)
    return values.astype(jnp.bfloat16)


def touch_ends(drawn, rng, least, top_value):
    place = [jax.random.randint(jax.random.fold_in(rng, axis), (), 0, length) for axis, length in enumerate(drawn.shape)]
    longest = drawn.shape.index(max(drawn.shape))
    next_to = place[:longest] + [(place[longest] + 1) % drawn.shape[longest]] + place[longest + 1:]
    return drawn.at[tuple(place)].set(least).at[tuple(next_to)].set(top_value)


def level_of(key, dims, pieces, low, largest):
    factor_of, own = 1.0, jax.random.fold_in(key, 6)
    for position, blocks in pieces:
        draws = jnp.exp(jax.random.uniform(jax.random.fold_in(own, position), (blocks,), jnp.float32, low / len(pieces), largest / len(pieces)))
        factor_of = factor_of * jnp.repeat(draws, dims[position] // blocks).reshape([-1 if axis == position else 1 for axis in range(len(dims))])
    return factor_of


def centred(stream_key, extent, spread, most, cuts=(), kind=jnp.bfloat16):
    result = jax.random.normal(stream_key, extent, jnp.float32) * spread
    if len(cuts) > 0:
        result = level_of(stream_key, extent, cuts, -0.22, 0.18) * result
    return jnp.clip(result, min=-most, max=most).astype(kind)


def setup_inputs(seed: int = 0) -> dict:
    seeds = jax.random.split(jax.random.key(seed), 11)
    return {
        "features": centred(seeds[0], (NODES, WIDTH), 1.0, 6.0, ((0, 16),)),
        "weight": centred(seeds[1], (WIDTH, WIDTH), WIDTH ** -0.5, 0.375),
        "bias": centred(seeds[2], (WIDTH,), 0.5, 3.0, (), jnp.float32),
        "cotangent": draw_cotangent(jax.random.fold_in(seeds[10], 71), 0),
        "tile_values": centred(seeds[4], (SLABS, SLABS, SLOTS, TILE, TILE), (TILE * SLABS * SLOTS // (2 * BLOCKS)) ** -0.5, 0.125, ((0, 16), (1, 2))),
        "tile_index": touch_ends(jax.random.randint(seeds[5], (SLABS, SLABS, SLOTS, 2), 0, BLOCKS), jax.random.fold_in(seeds[5], 1), 0, BLOCKS - 1).astype(jnp.int32),
        "tile_count": draw_tile_count(jax.random.fold_in(seeds[10], 71), 0),
        "rev_values": centred(seeds[7], (SLABS, SLABS, SLOTS, TILE, TILE), (TILE * SLABS * SLOTS // (2 * BLOCKS)) ** -0.5, 0.125, ((0, 16), (1, 2))),
        "rev_index": touch_ends(jax.random.randint(seeds[8], (SLABS, SLABS, SLOTS, 2), 0, BLOCKS), jax.random.fold_in(seeds[8], 1), 0, BLOCKS - 1).astype(jnp.int32),
        "rev_count": draw_rev_count(jax.random.fold_in(seeds[10], 71), 0),
    }


def apply_tiles(source, values, slot_index, counts):
    blocks = source.reshape(SLABS, BLOCKS, TILE, WIDTH)

    def one_slab(slab_id):
        tile_block = values[slab_id].astype(jnp.float32)
        slab_slots = slot_index[slab_id]
        slab_counts = counts[slab_id]
        partner = ((slab_id + jnp.arange(SLABS, dtype=jnp.int32)) % SLABS).astype(jnp.int32)
        sources = blocks[partner[:, None], slab_slots[:, :, 1]].astype(jnp.float32)
        product = jnp.einsum("dtab,dtbf->dtaf", tile_block, sources, precision=lax.Precision.HIGHEST)
        usable = jnp.arange(SLOTS, dtype=jnp.int32)[None, :] < slab_counts[:, None]
        placing = ((slab_slots[:, :, 0][:, :, None] == jnp.arange(BLOCKS, dtype=jnp.int32)[None, None, :]) & usable[:, :, None]).astype(jnp.float32)
        return jnp.einsum("dtn,dtaf->naf", placing, product, precision=lax.Precision.HIGHEST)

    summed = lax.map(one_slab, jnp.arange(SLABS, dtype=jnp.int32))
    return summed.reshape(NODES, WIDTH)


def reference(features, weight, bias, cotangent, tile_values, tile_index, tile_count, rev_values, rev_index, rev_count):
    mixed = apply_tiles(features, tile_values, tile_index, tile_count).astype(jnp.bfloat16)
    preact = jnp.dot(mixed, weight, preferred_element_type=jnp.float32) + bias
    sigmoid_pre = jax.nn.sigmoid(preact)
    activations = (preact * sigmoid_pre).astype(jnp.bfloat16)
    grad_pre = (cotangent.astype(jnp.float32) * sigmoid_pre * (1.0 + preact * (1.0 - sigmoid_pre))).astype(jnp.bfloat16)
    grad_scale = float(NODES) ** -0.5
    grad_weight = jnp.dot(mixed.T, grad_pre, preferred_element_type=jnp.float32) * grad_scale
    grad_bias = jnp.sum(grad_pre.astype(jnp.float32), axis=0) * grad_scale
    image = jnp.dot(grad_pre, weight.T, preferred_element_type=jnp.float32).astype(jnp.bfloat16)
    grad_features = apply_tiles(image, rev_values, rev_index, rev_count).astype(jnp.bfloat16)
    return (activations, grad_features, grad_weight, grad_bias)
```

```python
import functools

import jax
import jax.numpy as jnp
from jax import lax
from jax.experimental import pallas as pl
from jax.experimental.pallas import tpu as pltpu
from jax.sharding import PartitionSpec as P

TILE = 128
BLOCKS = 4
MESH = pl.DeviceIdType.MESH


def passed_along(value, axis, steps):
    count = lax.axis_size(axis)
    pairs = [(source, (source + steps) % count) for source in range(count)]
    return lax.ppermute(value, axis, pairs)


def section_term(current, tile_block, slot_index, counts):
    blocks = current.reshape(BLOCKS, TILE, current.shape[1])
    picks = (slot_index[:, 1][:, None] == jnp.arange(BLOCKS, dtype=jnp.int32)[None, :]).astype(jnp.bfloat16)
    sources = jnp.einsum("tn,nbf->tbf", picks, blocks, preferred_element_type=jnp.float32).astype(jnp.bfloat16)
    product = jnp.einsum("tab,tbf->taf", tile_block, sources, preferred_element_type=jnp.float32)
    usable = jnp.arange(slot_index.shape[0], dtype=jnp.int32) < counts
    placing = (
        (slot_index[:, 0][None, :] == jnp.arange(BLOCKS, dtype=jnp.int32)[:, None])
        & usable[None, :]
    ).astype(jnp.float32)
    return jnp.einsum("nt,taf->naf", placing, product, precision=lax.Precision.HIGHEST)


def first_source(source, sections):
    rep_index = lax.axis_index("rep")
    groups = lax.axis_size("rep")
    current = source
    for shift_bit in range(groups.bit_length() - 1):
        shifted = passed_along(current, "row", -(sections << shift_bit))
        current = jnp.where(rep_index >> shift_bit & 1 == 1, shifted, current)
    return current


def apply_tiles(source, values, slot_index, counts):
    sections = values.shape[1]
    current = first_source(source, sections)
    summed_rows = jnp.zeros((BLOCKS, TILE, source.shape[1]), jnp.float32)
    for section in range(sections):
        if section > 0:
            current = passed_along(current, "row", -1)
        summed_rows = summed_rows + section_term(
            current, values[0, section], slot_index[0, section], counts[0, section]
        )
    return summed_rows.reshape(source.shape[0], source.shape[1])


def own_rows(matrix):
    share_size = matrix.shape[0] // lax.axis_size("rep")
    return lax.dynamic_slice_in_dim(matrix, lax.axis_index("rep") * share_size, share_size, 0)


def activate(preact, cotangent):
    sigmoid_pre = jax.nn.sigmoid(preact)
    activations = (preact * sigmoid_pre).astype(jnp.bfloat16)
    grad_pre = (
        cotangent.astype(jnp.float32) * sigmoid_pre * (1.0 + preact * (1.0 - sigmoid_pre))
    ).astype(jnp.bfloat16)
    return (activations, grad_pre)


def general(
    features, weight, bias, cotangent, tile_values, tile_index, tile_count, rev_values, rev_index, rev_count
):
    node_total = features.shape[0] * lax.axis_size("row")
    grad_scale = float(node_total) ** (-0.5)
    summed = lax.psum(apply_tiles(features, tile_values, tile_index, tile_count), "rep")
    mixed_all = summed.astype(jnp.bfloat16)
    preact_all = jnp.dot(mixed_all, weight, preferred_element_type=jnp.float32) + bias
    cotangent_all = lax.all_gather(cotangent, "rep", axis=0, tiled=True)
    activ_all, grad_all = activate(preact_all, cotangent_all)
    image = jnp.einsum("ng,fg->nf", grad_all, weight, preferred_element_type=jnp.float32).astype(
        jnp.bfloat16
    )
    mixed_rows = own_rows(mixed_all)
    grad_pre = own_rows(grad_all)
    activations = own_rows(activ_all)
    weight_term = jnp.einsum("nf,ng->fg", mixed_rows, grad_pre, preferred_element_type=jnp.float32)
    bias_term = jnp.sum(grad_pre.astype(jnp.float32), axis=0)
    grad_weight, grad_bias = lax.psum((weight_term, bias_term), ("row", "rep"))
    back_rows = own_rows(lax.psum(apply_tiles(image, rev_values, rev_index, rev_count), "rep"))
    return (
        activations,
        back_rows.astype(jnp.bfloat16),
        grad_weight * grad_scale,
        grad_bias * grad_scale,
    )


SLABS = 16
SLOTS = 8
HALF = 256
WIDTH = 256
BLOCK = 136
PART = 72


def fused_kernel(
    scale,
    codes_ref, feat_ref, weight_ref, bias_ref, cot_ref, fwd_hbm, rev_hbm,
    act_ref, back_ref, gw_ref, gb_ref,
    gathered, tiles, codes_all, codes_s, acc, peer_acc,
    mixed_v, gpre_v, term, term_in, part_p, in_p, part_q, in_q, part_z, final,
    send_sem, recv_sem, tile_own, tile_send, tile_recv, code_sem, acc_send, acc_recv, red_send, red_recv,
):
    me, core = lax.axis_index("row"), lax.axis_index("rep")
    x, y, z = lax.rem(me, 2), lax.rem(lax.div(me, 2), 2), lax.div(me, 4)
    step_x, step_y = 1 - 2 * x, 2 - 4 * y
    other = 1 - core
    step_p = step_x * other + step_y * core
    step_q = step_x * core + step_y * other
    bit_p = x * other + y * core
    twin, peer_p, peer_q = (me, other), (me + step_p, core), (me + step_q, core)
    plane = lax.rem(me, 4)

    def line(k):
        return lax.rem(z + k, 4) * 4 + plane

    peers_z = [(line(k), core) for k in (1, 2, 3)]

    def remote(src, dst, s, r, dev):
        return pltpu.make_async_remote_copy(
            src_ref=src, dst_ref=dst, send_sem=s, recv_sem=r, device_id=dev, device_id_type=MESH
        )

    barrier = pltpu.get_barrier_semaphore()
    for dev in [twin, peer_p, peer_q] + peers_z:
        pl.semaphore_signal(barrier, inc=1, device_id=dev, device_id_type=MESH)
    gathered[0, me] = feat_ref[pl.ds(pl.multiple_of(core * HALF, HALF), HALF), :]
    pl.semaphore_wait(barrier, 6)

    def piece(phase, slab, sem, dev):
        return remote(
            gathered.at[phase, slab], gathered.at[phase, slab],
            send_sem.at[phase, sem], recv_sem.at[phase, slab], dev,
        )

    def send_own(phase):
        for k, dev in enumerate(peers_z):
            piece(phase, me, k, dev).start()
        piece(phase, me, 3, peer_p).start()
        piece(phase, me, 7, peer_q).start()

    def forward_line(phase):
        def body(k, carry):
            slab = line(k)
            piece(phase, slab, 0, peer_p).wait_recv()
            piece(phase, slab, 3 + k, peer_p).start()
            piece(phase, slab, 7 + k, peer_q).start()
            return carry
        lax.fori_loop(1, 4, body, 0)

    def term_of(phase, slab):
        offset = lax.rem(slab - me + SLABS, SLABS)
        group, within = lax.div(offset, 8), lax.rem(offset, 8)
        lefts, rights = [[] for _ in range(BLOCKS)], []
        low, high = gathered[phase, slab, 0:TILE, :], gathered[phase, slab, TILE:HALF, :]
        for t in range(SLOTS):
            code = codes_s[group, phase, within * SLOTS + t]
            second = jnp.where((code & 1) == 1, 1.0, 0.0).astype(jnp.float32)
            mine = ((code >> 1) & 1) == core
            value = tiles[phase, offset, t]
            rights.append(
                low * jnp.full(low.shape, 1.0 - second, jnp.float32).astype(jnp.bfloat16)
                + high * jnp.full(low.shape, second, jnp.float32).astype(jnp.bfloat16)
            )
            for n in range(BLOCKS):
                used = jnp.where(mine & ((code >> 2) == n), 1.0, 0.0).astype(jnp.float32)
                lefts[n].append(value * jnp.full((TILE, TILE), used, jnp.float32).astype(jnp.bfloat16))
        right = jnp.concatenate(rights, axis=0)
        for n in range(BLOCKS):
            acc[phase, n * TILE:(n + 1) * TILE, :] += jnp.dot(
                jnp.concatenate(lefts[n], axis=1), right, preferred_element_type=jnp.float32
            )

    def forward_p(phase):
        def body(k, carry):
            slab = line(k) + step_p
            piece(phase, slab, 0, peer_q).wait_recv()
            piece(phase, slab, 11 + k, peer_q).start()
            term_of(phase, line(k))
            return carry
        lax.fori_loop(0, 4, body, 0)

    def add_p(phase):
        def body(k, carry):
            term_of(phase, line(k) + step_p)
            return carry
        lax.fori_loop(0, 4, body, 0)

    def add_q(phase, first, last):
        def body(k, carry):
            slab = line(lax.rem(k, 4)) + step_p * lax.div(k, 4) + step_q
            piece(phase, slab, 0, peer_q).wait_recv()
            term_of(phase, slab)
            return carry
        lax.fori_loop(first, last, body, 0)

    own_half = pl.ds(pl.multiple_of(core * HALF, HALF), HALF)
    twin_half = pl.ds(pl.multiple_of(other * HALF, HALF), HALF)

    def swap_acc(phase):
        copy = remote(
            acc.at[phase, twin_half], peer_acc.at[phase], acc_send.at[phase], acc_recv.at[phase], twin
        )
        copy.start()
        copy.wait()
        return acc[phase, own_half, :] + peer_acc[phase]

    def tile_copies(phase, source):
        place = pl.ds(core * 8, 8)
        return (
            pltpu.make_async_copy(source.at[0], tiles.at[phase, place], tile_own.at[phase]),
            remote(source.at[0], tiles.at[phase, place], tile_send.at[phase], tile_recv.at[phase], twin),
        )

    send_own(0)
    codes_all[core] = codes_ref[...]
    code_copy = remote(codes_all.at[core], codes_all.at[core], code_sem.at[0], code_sem.at[1], twin)
    code_copy.start()
    near, far = tile_copies(0, fwd_hbm)
    near.start()
    far.start()
    acc[...] = jnp.zeros_like(acc)
    forward_line(0)
    code_copy.wait()
    to_scalar = pltpu.make_async_copy(codes_all, codes_s, code_sem.at[2])
    to_scalar.start()
    to_scalar.wait()
    near.wait()
    far.wait()
    near, far = tile_copies(1, rev_hbm)
    near.start()
    far.start()
    forward_p(0)
    add_p(0)
    add_q(0, 0, 8)

    mixed = swap_acc(0).astype(jnp.bfloat16)
    mixed_v[...] = mixed
    preact = jnp.dot(mixed, weight_ref[...], preferred_element_type=jnp.float32) + bias_ref[...]
    sigmoid = jax.nn.sigmoid(preact)
    act_ref[...] = (preact * sigmoid).astype(jnp.bfloat16)
    gpre_v[...] = (
        cot_ref[...].astype(jnp.float32) * sigmoid * (1.0 + preact * (1.0 - sigmoid))
    ).astype(jnp.bfloat16)
    gathered[1, me] = lax.dot_general(
        gpre_v[...], weight_ref[...], (((1,), (1,)), ((), ())), preferred_element_type=jnp.float32
    ).astype(jnp.bfloat16)
    send_own(1)

    whole = lax.dot_general(
        mixed_v[...], gpre_v[...], (((0,), (0,)), ((), ())), preferred_element_type=jnp.float32
    )
    sums = jnp.sum(gpre_v[...].astype(jnp.float32).reshape(HALF // 8, 8, WIDTH), axis=0)
    for h in range(2):
        term[h, 0:64, :] = whole[128 * h:128 * h + 64]
        term[h, 64:72, :] = sums
        term[h, 72:136, :] = whole[128 * h + 64:128 * h + 128]
    to_twin = remote(term.at[other], term_in, red_send.at[0], red_recv.at[0], twin)
    to_twin.start()
    forward_line(1)
    near.wait()
    far.wait()
    to_twin.wait()
    part_p[...] = term[core] + term_in[...]
    keep = pl.ds(pl.multiple_of(bit_p * 64, 8), PART)
    give = pl.ds(pl.multiple_of((1 - bit_p) * 64, 8), PART)
    to_p = remote(part_p.at[give], in_p, red_send.at[1], red_recv.at[1], peer_p)
    to_p.start()
    forward_p(1)
    to_p.wait()
    part_q[...] = part_p[keep, :] + in_p[...]
    to_q = remote(part_q, in_q, red_send.at[2], red_recv.at[2], peer_q)
    to_q.start()
    add_p(1)
    to_q.wait()
    part_z[z] = part_q[...] + in_q[...]
    to_z = [
        remote(part_z.at[z], part_z.at[z], red_send.at[3 + k], red_recv.at[3 + z], dev)
        for k, dev in enumerate(peers_z)
    ]
    for copy in to_z:
        copy.start()
    add_q(1, 0, 4)
    for k in (1, 2, 3):
        at = lax.rem(z + k, 4)
        remote(part_z.at[at], part_z.at[at], red_send.at[3], red_recv.at[3 + at], twin).wait_recv()
    final[core, keep, :] = ((part_z[0] + part_z[1]) + part_z[2]) + part_z[3]
    up = final.at[core, pl.ds(pl.multiple_of(bit_p * PART, 8), 64)]
    up_p = remote(up, up, red_send.at[6], red_recv.at[7], peer_p)
    up_p.start()
    add_q(1, 4, 6)
    up_p.wait()
    up_twin = remote(final.at[core], final.at[core], red_send.at[7], red_recv.at[8], twin)
    up_twin.start()
    add_q(1, 6, 8)
    copy = remote(acc.at[1, twin_half], peer_acc.at[1], acc_send.at[1], acc_recv.at[1], twin)
    copy.start()
    up_twin.wait()
    for h in range(2):
        gw_ref[128 * h:128 * h + 64, :] = final[h, 0:64, :] * scale
        gw_ref[128 * h + 64:128 * h + 128, :] = final[h, 72:136, :] * scale
    gb_ref[...] = jnp.sum(final[0, 64:72, :], axis=0, keepdims=True) * scale
    copy.wait()
    back_ref[...] = (acc[1, own_half, :] + peer_acc[1]).astype(jnp.bfloat16)
    for k in range(3):
        to_z[k].wait_send()
    for phase in range(2):
        def drain(k, carry):
            piece(phase, me, k, twin).wait_send()
            return carry
        lax.fori_loop(0, 15, drain, 0)


def codes_of(index, count):
    slot = jnp.arange(index.shape[2], dtype=jnp.int32)[None, :]
    code = index[0, :, :, 0] * BLOCKS + index[0, :, :, 1]
    return jnp.where(slot < count[0][:, None], code, 4 * BLOCKS * BLOCKS).reshape(1, -1)


def fused(
    features, weight, bias, cotangent, tile_values, tile_index, tile_count, rev_values, rev_index, rev_count
):
    scale = float(features.shape[0] * lax.axis_size("row")) ** (-0.5)
    codes = jnp.concatenate([codes_of(tile_index, tile_count), codes_of(rev_index, rev_count)], axis=0)
    codes = jnp.pad(codes, ((0, 6), (0, 128 - codes.shape[1])))
    vmem = pl.BlockSpec(memory_space=pltpu.VMEM)
    anywhere = pl.BlockSpec(memory_space=pl.ANY)
    f32, bf16 = jnp.float32, jnp.bfloat16
    act, back, gw, gb = pl.pallas_call(
        functools.partial(fused_kernel, scale),
        out_shape=(
            jax.ShapeDtypeStruct((HALF, WIDTH), bf16),
            jax.ShapeDtypeStruct((HALF, WIDTH), bf16),
            jax.ShapeDtypeStruct((WIDTH, WIDTH), f32),
            jax.ShapeDtypeStruct((1, WIDTH), f32),
        ),
        in_specs=[vmem] * 5 + [anywhere] * 2,
        out_specs=(vmem,) * 4,
        scratch_shapes=[
            pltpu.VMEM((2, SLABS, HALF, WIDTH), bf16),
            pltpu.VMEM((2, SLABS, SLOTS, TILE, TILE), bf16),
            pltpu.VMEM((2, 8, 128), jnp.int32),
            pltpu.SMEM((2, 8, 128), jnp.int32),
            pltpu.VMEM((2, 2 * HALF, WIDTH), f32),
            pltpu.VMEM((2, HALF, WIDTH), f32),
            pltpu.VMEM((HALF, WIDTH), bf16),
            pltpu.VMEM((HALF, WIDTH), bf16),
            pltpu.VMEM((2, BLOCK, WIDTH), f32),
            pltpu.VMEM((BLOCK, WIDTH), f32),
            pltpu.VMEM((BLOCK, WIDTH), f32),
            pltpu.VMEM((PART, WIDTH), f32),
            pltpu.VMEM((PART, WIDTH), f32),
            pltpu.VMEM((PART, WIDTH), f32),
            pltpu.VMEM((4, PART, WIDTH), f32),
            pltpu.VMEM((2, BLOCK, WIDTH), f32),
            pltpu.SemaphoreType.DMA((2, 15)),
            pltpu.SemaphoreType.DMA((2, SLABS)),
            pltpu.SemaphoreType.DMA((2,)),
            pltpu.SemaphoreType.DMA((2,)),
            pltpu.SemaphoreType.DMA((2,)),
            pltpu.SemaphoreType.DMA((3,)),
            pltpu.SemaphoreType.DMA((2,)),
            pltpu.SemaphoreType.DMA((2,)),
            pltpu.SemaphoreType.DMA((8,)),
            pltpu.SemaphoreType.DMA((9,)),
        ],
        compiler_params=pltpu.CompilerParams(
            collective_id=0, has_side_effects=True, vmem_limit_bytes=40 * 2**20
        ),
    )(codes, features, weight, bias[None, :], cotangent, tile_values, rev_values)
    return act, back, gw, gb[0]


def solution(mesh):
    placed = (
        P("row", None),
        P(),
        P(),
        P(("row", "rep"), None),
        P("row", "rep", None, None, None),
        P("row", "rep", None, None),
        P("row", "rep"),
        P("row", "rep", None, None, None),
        P("row", "rep", None, None),
        P("row", "rep"),
    )
    pairs = mesh.shape["row"] == SLABS and mesh.shape["rep"] == 2
    return jax.shard_map(
        fused if pairs else general,
        mesh=mesh,
        in_specs=placed,
        out_specs=(P(("row", "rep"), None), P(("row", "rep"), None), P(), P()),
        check_vma=False,
    )
```

```python
import functools

import jax
import jax.numpy as jnp
from jax import lax
from jax.experimental import pallas as pl
from jax.experimental.pallas import tpu as pltpu
from jax.sharding import PartitionSpec as P

TILE = 128
BLOCKS = 4
MESH = pl.DeviceIdType.MESH


def passed_along(value, axis, steps):
    count = lax.axis_size(axis)
    pairs = [(source, (source + steps) % count) for source in range(count)]
    return lax.ppermute(value, axis, pairs)


def section_term(current, tile_block, slot_index, counts):
    blocks = current.reshape(BLOCKS, TILE, current.shape[1])
    picks = (slot_index[:, 1][:, None] == jnp.arange(BLOCKS, dtype=jnp.int32)[None, :]).astype(jnp.bfloat16)
    sources = jnp.einsum("tn,nbf->tbf", picks, blocks, preferred_element_type=jnp.float32).astype(jnp.bfloat16)
    product = jnp.einsum("tab,tbf->taf", tile_block, sources, preferred_element_type=jnp.float32)
    usable = jnp.arange(slot_index.shape[0], dtype=jnp.int32) < counts
    placing = (
        (slot_index[:, 0][None, :] == jnp.arange(BLOCKS, dtype=jnp.int32)[:, None])
        & usable[None, :]
    ).astype(jnp.float32)
    return jnp.einsum("nt,taf->naf", placing, product, precision=lax.Precision.HIGHEST)


def first_source(source, sections):
    rep_index = lax.axis_index("rep")
    groups = lax.axis_size("rep")
    current = source
    for shift_bit in range(groups.bit_length() - 1):
        shifted = passed_along(current, "row", -(sections << shift_bit))
        current = jnp.where(rep_index >> shift_bit & 1 == 1, shifted, current)
    return current


def apply_tiles(source, values, slot_index, counts):
    sections = values.shape[1]
    current = first_source(source, sections)
    summed_rows = jnp.zeros((BLOCKS, TILE, source.shape[1]), jnp.float32)
    for section in range(sections):
        if section > 0:
            current = passed_along(current, "row", -1)
        summed_rows = summed_rows + section_term(
            current, values[0, section], slot_index[0, section], counts[0, section]
        )
    return summed_rows.reshape(source.shape[0], source.shape[1])


def own_rows(matrix):
    share_size = matrix.shape[0] // lax.axis_size("rep")
    return lax.dynamic_slice_in_dim(matrix, lax.axis_index("rep") * share_size, share_size, 0)


def activate(preact, cotangent):
    sigmoid_pre = jax.nn.sigmoid(preact)
    activations = (preact * sigmoid_pre).astype(jnp.bfloat16)
    grad_pre = (
        cotangent.astype(jnp.float32) * sigmoid_pre * (1.0 + preact * (1.0 - sigmoid_pre))
    ).astype(jnp.bfloat16)
    return (activations, grad_pre)


def general(
    features, weight, bias, cotangent, tile_values, tile_index, tile_count, rev_values, rev_index, rev_count
):
    node_total = features.shape[0] * lax.axis_size("row")
    grad_scale = float(node_total) ** (-0.5)
    summed = lax.psum(apply_tiles(features, tile_values, tile_index, tile_count), "rep")
    mixed_all = summed.astype(jnp.bfloat16)
    preact_all = jnp.dot(mixed_all, weight, preferred_element_type=jnp.float32) + bias
    cotangent_all = lax.all_gather(cotangent, "rep", axis=0, tiled=True)
    activ_all, grad_all = activate(preact_all, cotangent_all)
    image = jnp.einsum("ng,fg->nf", grad_all, weight, preferred_element_type=jnp.float32).astype(
        jnp.bfloat16
    )
    mixed_rows = own_rows(mixed_all)
    grad_pre = own_rows(grad_all)
    activations = own_rows(activ_all)
    weight_term = jnp.einsum("nf,ng->fg", mixed_rows, grad_pre, preferred_element_type=jnp.float32)
    bias_term = jnp.sum(grad_pre.astype(jnp.float32), axis=0)
    grad_weight, grad_bias = lax.psum((weight_term, bias_term), ("row", "rep"))
    back_rows = own_rows(lax.psum(apply_tiles(image, rev_values, rev_index, rev_count), "rep"))
    return (
        activations,
        back_rows.astype(jnp.bfloat16),
        grad_weight * grad_scale,
        grad_bias * grad_scale,
    )


SLABS = 16
SLOTS = 8
HALF = 256
WIDTH = 256
BLOCK = 136
PART = 72


def fused_kernel(
    scale,
    codes_ref, feat_hbm, weight_hbm, bias_hbm, cot_hbm, fwd_hbm, rev_hbm,
    act_ref, back_ref, gw_ref, gb_ref,
    weight_ref, bias_ref, cot_ref, load_sem,
    gathered, tiles, codes_all, codes_s, acc, peer_acc,
    mixed_v, gpre_v, term, term_in, part_p, in_p, part_q, in_q, part_z, final,
    send_sem, recv_sem, tile_own, tile_send, tile_recv, code_sem, acc_send, acc_recv, red_send, red_recv,
):
    me, core = lax.axis_index("row"), lax.axis_index("rep")
    x, y, z = lax.rem(me, 2), lax.rem(lax.div(me, 2), 2), lax.div(me, 4)
    step_x, step_y = 1 - 2 * x, 2 - 4 * y
    other = 1 - core
    step_p = step_x * other + step_y * core
    step_q = step_x * core + step_y * other
    bit_p = x * other + y * core
    twin, peer_p, peer_q = (me, other), (me + step_p, core), (me + step_q, core)
    plane = lax.rem(me, 4)

    inner = lax.div(z * (3 - z), 2)
    toward = 1 - 2 * lax.div(z, 2)

    def level(k):
        return z + toward * (k * (1 - inner) + inner * lax.div(k + 1, 2) * (2 * lax.rem(k, 2) - 1))

    def line(k):
        return level(k) * 4 + plane

    peers_z = [(lax.rem(z + k, 4) * 4 + plane, core) for k in (1, 2, 3)]
    above, below = (me + 4, core), (me - 4, core)

    def remote(src, dst, s, r, dev):
        return pltpu.make_async_remote_copy(
            src_ref=src, dst_ref=dst, send_sem=s, recv_sem=r, device_id=dev, device_id_type=MESH
        )

    barrier = pltpu.get_barrier_semaphore()
    for dev in [twin, peer_p, peer_q] + peers_z:
        pl.semaphore_signal(barrier, inc=1, device_id=dev, device_id_type=MESH)
    own_half = pl.ds(pl.multiple_of(core * HALF, HALF), HALF)
    twin_half = pl.ds(pl.multiple_of(other * HALF, HALF), HALF)
    loads = [
        pltpu.make_async_copy(src, dst, load_sem.at[i])
        for i, (src, dst) in enumerate(
            [
                (feat_hbm.at[own_half], gathered.at[0, me]),
                (weight_hbm, weight_ref),
                (bias_hbm, bias_ref),
                (cot_hbm, cot_ref),
            ]
        )
    ]
    for load in loads:
        load.start()
    loads[0].wait()
    pl.semaphore_wait(barrier, 6)

    def piece(phase, slab, sem, dev):
        return remote(
            gathered.at[phase, slab], gathered.at[phase, slab],
            send_sem.at[phase, sem], recv_sem.at[phase, slab], dev,
        )

    def send_own(phase):
        @pl.when(z < 3)
        def _():
            piece(phase, me, 12 + z, above).start()

        @pl.when(z > 0)
        def _():
            piece(phase, me, 16 + z, below).start()

        piece(phase, me, 0, peer_p).start()
        piece(phase, me, 4, peer_q).start()

    def forward_line(phase, first, last):
        def body(k, carry):
            at, slab = level(k), line(k)
            piece(phase, slab, 0, peer_p).wait_recv()

            @pl.when((at < z) & (z < 3))
            def _():
                piece(phase, slab, 12 + at, above).start()

            @pl.when((at > z) & (z > 0))
            def _():
                piece(phase, slab, 16 + at, below).start()

            piece(phase, slab, k, peer_p).start()
            piece(phase, slab, 4 + k, peer_q).start()
            return carry
        lax.fori_loop(first, last, body, 0)

    def term_of(phase, slab):
        offset = lax.rem(slab - me + SLABS, SLABS)
        group, within = lax.div(offset, 8), lax.rem(offset, 8)
        lefts, rights = [[] for _ in range(BLOCKS)], []
        low, high = gathered[phase, slab, 0:TILE, :], gathered[phase, slab, TILE:HALF, :]
        for t in range(SLOTS):
            code = codes_s[group, phase, within * SLOTS + t]
            second = jnp.where((code & 1) == 1, 1.0, 0.0).astype(jnp.float32)
            mine = ((code >> 1) & 1) == core
            value = tiles[phase, offset, t]
            rights.append(
                low * jnp.full(low.shape, 1.0 - second, jnp.float32).astype(jnp.bfloat16)
                + high * jnp.full(low.shape, second, jnp.float32).astype(jnp.bfloat16)
            )
            for n in range(BLOCKS):
                used = jnp.where(mine & ((code >> 2) == n), 1.0, 0.0).astype(jnp.float32)
                lefts[n].append(value * jnp.full((TILE, TILE), used, jnp.float32).astype(jnp.bfloat16))
        right = jnp.concatenate(rights, axis=0)
        for n in range(BLOCKS):
            acc[phase, n * TILE:(n + 1) * TILE, :] += jnp.dot(
                jnp.concatenate(lefts[n], axis=1), right, preferred_element_type=jnp.float32
            )

    def forward_p(phase, first, last):
        def body(k, carry):
            slab = line(k) + step_p
            piece(phase, slab, 0, peer_q).wait_recv()
            piece(phase, slab, 8 + k, peer_q).start()
            term_of(phase, line(k))
            return carry
        lax.fori_loop(first, last, body, 0)

    def add_p(phase):
        def body(k, carry):
            term_of(phase, line(k) + step_p)
            return carry
        lax.fori_loop(0, 4, body, 0)

    def add_q(phase, first, last):
        def body(k, carry):
            slab = line(lax.rem(k, 4)) + step_p * lax.div(k, 4) + step_q
            piece(phase, slab, 0, peer_q).wait_recv()
            term_of(phase, slab)
            return carry
        lax.fori_loop(first, last, body, 0)

    def swap_acc(phase):
        copy = remote(
            acc.at[phase, twin_half], peer_acc.at[phase], acc_send.at[phase], acc_recv.at[phase], twin
        )
        copy.start()
        copy.wait()
        return acc[phase, own_half, :] + peer_acc[phase]

    def tile_copies(phase, source):
        place = pl.ds(core * 8, 8)
        return (
            pltpu.make_async_copy(source.at[0], tiles.at[phase, place], tile_own.at[phase]),
            remote(source.at[0], tiles.at[phase, place], tile_send.at[phase], tile_recv.at[phase], twin),
        )

    send_own(0)
    codes_all[core] = codes_ref[...]
    code_copy = remote(codes_all.at[core], codes_all.at[core], code_sem.at[0], code_sem.at[1], twin)
    code_copy.start()
    near, far = tile_copies(0, fwd_hbm)
    near.start()
    far.start()
    acc[...] = jnp.zeros_like(acc)
    forward_line(0, 1, 4)
    code_copy.wait()
    to_scalar = pltpu.make_async_copy(codes_all, codes_s, code_sem.at[2])
    to_scalar.start()
    to_scalar.wait()
    near.wait()
    far.wait()
    near, far = tile_copies(1, rev_hbm)
    near.start()
    far.start()
    forward_p(0, 0, 4)
    add_p(0)
    add_q(0, 0, 8)

    for load in loads[1:]:
        load.wait()
    mixed = swap_acc(0).astype(jnp.bfloat16)
    mixed_v[...] = mixed
    preact = jnp.dot(mixed, weight_ref[...], preferred_element_type=jnp.float32) + bias_ref[...]
    sigmoid = jax.nn.sigmoid(preact)
    act_ref[...] = (preact * sigmoid).astype(jnp.bfloat16)
    gpre_v[...] = (
        cot_ref[...].astype(jnp.float32) * sigmoid * (1.0 + preact * (1.0 - sigmoid))
    ).astype(jnp.bfloat16)
    gathered[1, me] = lax.dot_general(
        gpre_v[...], weight_ref[...], (((1,), (1,)), ((), ())), preferred_element_type=jnp.float32
    ).astype(jnp.bfloat16)
    send_own(1)

    whole = lax.dot_general(
        mixed_v[...], gpre_v[...], (((0,), (0,)), ((), ())), preferred_element_type=jnp.float32
    )
    sums = jnp.sum(gpre_v[...].astype(jnp.float32).reshape(HALF // 8, 8, WIDTH), axis=0)
    for h in range(2):
        term[h, 0:64, :] = whole[128 * h:128 * h + 64]
        term[h, 64:72, :] = sums
        term[h, 72:136, :] = whole[128 * h + 64:128 * h + 128]
    to_twin = remote(term.at[other], term_in, red_send.at[0], red_recv.at[0], twin)
    to_twin.start()
    near.wait()
    far.wait()
    to_twin.wait()
    part_p[...] = term[core] + term_in[...]
    keep = pl.ds(pl.multiple_of(bit_p * 64, 8), PART)
    give = pl.ds(pl.multiple_of((1 - bit_p) * 64, 8), PART)
    to_p = remote(part_p.at[give], in_p, red_send.at[1], red_recv.at[1], peer_p)
    to_p.start()
    forward_line(1, 1, 2)
    to_p.wait()
    part_q[...] = part_p[keep, :] + in_p[...]
    to_q = remote(part_q, in_q, red_send.at[2], red_recv.at[2], peer_q)
    to_q.start()
    forward_line(1, 2, 4)
    to_q.wait()
    part_z[z] = part_q[...] + in_q[...]
    to_z = [
        remote(part_z.at[z], part_z.at[z], red_send.at[3 + k], red_recv.at[3 + z], dev)
        for k, dev in enumerate(peers_z)
    ]
    for copy in to_z:
        copy.start()
    forward_p(1, 0, 4)
    for k in (1, 2, 3):
        at = lax.rem(z + k, 4)
        remote(part_z.at[at], part_z.at[at], red_send.at[3], red_recv.at[3 + at], twin).wait_recv()
    final[core, keep, :] = ((part_z[0] + part_z[1]) + part_z[2]) + part_z[3]
    up = final.at[core, pl.ds(pl.multiple_of(bit_p * PART, 8), 64)]
    up_p = remote(up, up, red_send.at[6], red_recv.at[7], peer_p)
    up_p.start()
    add_p(1)
    add_q(1, 0, 4)
    up_p.wait()
    up_twin = remote(final.at[core], final.at[core], red_send.at[7], red_recv.at[8], twin)
    up_twin.start()
    add_q(1, 4, 8)
    copy = remote(acc.at[1, twin_half], peer_acc.at[1], acc_send.at[1], acc_recv.at[1], twin)
    copy.start()
    up_twin.wait()
    for h in range(2):
        gw_ref[128 * h:128 * h + 64, :] = final[h, 0:64, :] * scale
        gw_ref[128 * h + 64:128 * h + 128, :] = final[h, 72:136, :] * scale
    gb_ref[...] = jnp.sum(final[0, 64:72, :], axis=0, keepdims=True) * scale
    copy.wait()
    back_ref[...] = (acc[1, own_half, :] + peer_acc[1]).astype(jnp.bfloat16)
    for k in range(3):
        to_z[k].wait_send()
    for phase in range(2):
        def drain(k, carry):
            piece(phase, me, k, twin).wait_send()
            return carry
        lax.fori_loop(0, 12, drain, 0)
        for at in range(4):
            @pl.when((z < 3) & (at <= z))
            def _():
                piece(phase, me, 12 + at, twin).wait_send()

            @pl.when((z > 0) & (at >= z))
            def _():
                piece(phase, me, 16 + at, twin).wait_send()


def codes_of(index, count):
    slot = jnp.arange(index.shape[2], dtype=jnp.int32)[None, :]
    code = index[0, :, :, 0] * BLOCKS + index[0, :, :, 1]
    return jnp.where(slot < count[0][:, None], code, 4 * BLOCKS * BLOCKS).reshape(1, -1)


def fused(
    features, weight, bias, cotangent, tile_values, tile_index, tile_count, rev_values, rev_index, rev_count
):
    scale = float(features.shape[0] * lax.axis_size("row")) ** (-0.5)
    codes = jnp.concatenate([codes_of(tile_index, tile_count), codes_of(rev_index, rev_count)], axis=0)
    codes = jnp.pad(codes, ((0, 6), (0, 128 - codes.shape[1])))
    vmem = pl.BlockSpec(memory_space=pltpu.VMEM)
    anywhere = pl.BlockSpec(memory_space=pl.ANY)
    f32, bf16 = jnp.float32, jnp.bfloat16
    act, back, gw, gb = pl.pallas_call(
        functools.partial(fused_kernel, scale),
        out_shape=(
            jax.ShapeDtypeStruct((HALF, WIDTH), bf16),
            jax.ShapeDtypeStruct((HALF, WIDTH), bf16),
            jax.ShapeDtypeStruct((WIDTH, WIDTH), f32),
            jax.ShapeDtypeStruct((1, WIDTH), f32),
        ),
        in_specs=[vmem] + [anywhere] * 6,
        out_specs=(vmem,) * 4,
        scratch_shapes=[
            pltpu.VMEM((WIDTH, WIDTH), bf16),
            pltpu.VMEM((1, WIDTH), f32),
            pltpu.VMEM((HALF, WIDTH), bf16),
            pltpu.SemaphoreType.DMA((4,)),
            pltpu.VMEM((2, SLABS, HALF, WIDTH), bf16),
            pltpu.VMEM((2, SLABS, SLOTS, TILE, TILE), bf16),
            pltpu.VMEM((2, 8, 128), jnp.int32),
            pltpu.SMEM((2, 8, 128), jnp.int32),
            pltpu.VMEM((2, 2 * HALF, WIDTH), f32),
            pltpu.VMEM((2, HALF, WIDTH), f32),
            pltpu.VMEM((HALF, WIDTH), bf16),
            pltpu.VMEM((HALF, WIDTH), bf16),
            pltpu.VMEM((2, BLOCK, WIDTH), f32),
            pltpu.VMEM((BLOCK, WIDTH), f32),
            pltpu.VMEM((BLOCK, WIDTH), f32),
            pltpu.VMEM((PART, WIDTH), f32),
            pltpu.VMEM((PART, WIDTH), f32),
            pltpu.VMEM((PART, WIDTH), f32),
            pltpu.VMEM((4, PART, WIDTH), f32),
            pltpu.VMEM((2, BLOCK, WIDTH), f32),
            pltpu.SemaphoreType.DMA((2, 20)),
            pltpu.SemaphoreType.DMA((2, SLABS)),
            pltpu.SemaphoreType.DMA((2,)),
            pltpu.SemaphoreType.DMA((2,)),
            pltpu.SemaphoreType.DMA((2,)),
            pltpu.SemaphoreType.DMA((3,)),
            pltpu.SemaphoreType.DMA((2,)),
            pltpu.SemaphoreType.DMA((2,)),
            pltpu.SemaphoreType.DMA((8,)),
            pltpu.SemaphoreType.DMA((9,)),
        ],
        compiler_params=pltpu.CompilerParams(
            collective_id=0, has_side_effects=True, vmem_limit_bytes=60 * 2**20
        ),
    )(codes, features, weight, bias[None, :], cotangent, tile_values, rev_values)
    return act, back, gw, gb[0]


def solution(mesh):
    placed = (
        P("row", None),
        P(),
        P(),
        P(("row", "rep"), None),
        P("row", "rep", None, None, None),
        P("row", "rep", None, None),
        P("row", "rep"),
        P("row", "rep", None, None, None),
        P("row", "rep", None, None),
        P("row", "rep"),
    )
    pairs = mesh.shape["row"] == SLABS and mesh.shape["rep"] == 2
    return jax.shard_map(
        fused if pairs else general,
        mesh=mesh,
        in_specs=placed,
        out_specs=(P(("row", "rep"), None), P(("row", "rep"), None), P(), P()),
        check_vma=False,
    )
```
